32 devices in a mesh: groups: 2 (over y), row: 4 (over z), col: 4 (over x, core).
Axes of the slice: x: 2, y: 2, z: 4, core: 2. Of those that a mesh axis runs over, the one named last changes fastest.
Arguments:
- grads_now: float32 [3072, 8192], P(('groups', 'col'), 'row'), parts along dimension 0, as said below
- grads_later: float32 [3072, 8192], P(('groups', 'row'), 'col'), parts along dimension 0, as said below
Outputs:
- covariance: float32 [16384, 8192], P(('groups', 'row'), 'col'), parts along dimension 0
There are 2 independent parts, one for each index of `groups`. The reference program is written for one: setup_inputs(seed, part) draws one part's arguments, and reference() takes and returns one part's arrays. A program takes and returns all parts, laid end to end along the dimension named above; each array names one. Nothing has to cross between parts.
Inputs may be any that keep to these rules, and one draw needn't show every extreme that they name: `grads_now`: gradients of two checkpoints of one model; per-feature scales differ. `grads_later`: gradients at the later checkpoint, correlated with those at checkpoint t.
All inputs are finite; a program needn't handle non-finite values.
Results may differ from the reference program's by a relative error of at most 0.00015.
Values sent between devices are 32-bit elements; how exact they have to be, the bound alone decides.
A program may use at most 128 MiB of HBM per device.

```python
import jax
import jax.numpy as jnp
from jax import lax

FEAT = 8192
N = 1536


def shared_noise(key):
    return jax.random.normal(jax.random.fold_in(key, 11), (N, FEAT), jnp.float32)


def feature_scales(key, low, high):
    return jnp.exp(jax.random.uniform(key, (1, FEAT), jnp.float32, jnp.log(low), jnp.log(high)))


def draw_grads_now(key, part):
    common = shared_noise(key)
    key = jax.random.fold_in(key, 1)
    scales = feature_scales(jax.random.fold_in(key, 2), 1.0, 3.0)
    return scales * common


def draw_grads_later(key, part):
    common = shared_noise(key)
    key = jax.random.fold_in(key, 5)
    fresh = jax.random.normal(jax.random.fold_in(key, 6), (N, FEAT), jnp.float32)
    scales = feature_scales(jax.random.fold_in(key, 7), 1.0, 3.0)
    return scales * (0.5 * common + fresh)


def setup_inputs(seed: int = 0, part: int = 0) -> dict:
    seeds = jax.random.split(jax.random.key(seed), 3)
    part_splits = jax.random.split(jax.random.fold_in(seeds[2], part), 3)
    grads_now = draw_grads_now(jax.random.fold_in(jax.random.fold_in(seeds[2], part), 71), part)
    grads_later = draw_grads_later(jax.random.fold_in(jax.random.fold_in(seeds[2], part), 71), part)
    return {"grads_now": grads_now, "grads_later": grads_later}


def reference(grads_now, grads_later):
    mean_now = jnp.mean(grads_now, axis=0, keepdims=True)
    centered_now = grads_now - mean_now
    product = lax.dot_general(centered_now, grads_later, (((0,), (0,)), ((), ())), precision=lax.Precision.HIGHEST, preferred_element_type=jnp.float32)
    return product / jnp.float32(N - 1)
```

```python
import functools

import jax
import jax.numpy as jnp
from jax import lax
from jax.experimental import pallas as pl
from jax.experimental.pallas import tpu as pltpu
from jax.sharding import PartitionSpec as P

MESH = pl.DeviceIdType.MESH
CHUNKS = 4
TILE = 256


def contract(left, right):
    return lax.dot_general(
        left,
        right,
        (((0,), (0,)), ((), ())),
        precision=lax.Precision.HIGHEST,
        preferred_element_type=jnp.float32,
    )


def split(x):
    high = x.astype(jnp.bfloat16)
    low = (x - high.astype(jnp.float32)).astype(jnp.bfloat16)
    return high, low


def kernel(
    n, now_ref, later_ref, out_ref,
    acc, lhs, rhs, held,
    own_now, own_later, now_send, now_recv, z_send, z_recv, out_sem,
):
    r, c = lax.axis_index("row"), lax.axis_index("col")
    rows, feats = now_ref.shape
    cols = later_ref.shape[1]
    width = cols // CHUNKS
    piece = rows // CHUNKS
    count = 4 * rows
    partner = c + 1 - 2 * (c % 2)
    across = (c + 2) % 4
    last = lax.max(r, n - 1 - r)

    def slot(block, ch):
        start = pl.multiple_of(block * rows + ch * piece, piece)
        return acc.at[pl.ds(start, piece), :]

    def columns(ch):
        return pl.ds(pl.multiple_of(ch * width, width), width)

    def now_copy(kind, ch, src, block, target):
        return pltpu.make_async_remote_copy(
            src_ref=src,
            dst_ref=slot(block, ch),
            send_sem=now_send.at[kind, ch],
            recv_sem=now_recv.at[kind, ch],
            device_id={"col": target},
            device_id_type=MESH,
        )

    def own_piece(ch):
        return now_ref.at[pl.ds(pl.multiple_of(ch * piece, piece), piece), :]

    def line_copy(side, origin, ch, src, target):
        return pltpu.make_async_remote_copy(
            src_ref=src,
            dst_ref=held.at[origin, ch],
            send_sem=z_send.at[side, origin, ch],
            recv_sem=z_recv.at[origin, ch],
            device_id={"row": target},
            device_id_type=MESH,
        )

    def in_line(i):
        return (i >= 0) & (i < n)

    def own_later_copy(ch):
        return pltpu.make_async_copy(later_ref.at[:, columns(ch)], held.at[r, ch], own_later.at[ch])

    def out_copy(ch):
        return pltpu.make_async_copy(acc.at[:, columns(ch)], out_ref.at[:, columns(ch)], out_sem.at[ch])

    barrier = pltpu.get_barrier_semaphore()
    pl.semaphore_signal(barrier, inc=1, device_id={"col": partner}, device_id_type=MESH)
    pl.semaphore_signal(barrier, inc=1, device_id={"col": across}, device_id_type=MESH)
    for side in range(2):
        target = r - 1 + 2 * side

        @pl.when(in_line(target))
        def _():
            pl.semaphore_signal(barrier, inc=1, device_id={"row": target}, device_id_type=MESH)

    pl.semaphore_wait(barrier, 2 + (r > 0).astype(jnp.int32) + (r < n - 1).astype(jnp.int32))

    def start_own(ch, carry):
        for side in range(2):
            target = r - 1 + 2 * side

            @pl.when(in_line(target))
            def _():
                line_copy(side, r, ch, later_ref.at[:, columns(ch)], target).start()

        now_copy(1, ch, own_piece(ch), c, across).start()
        now_copy(0, ch, own_piece(ch), c, partner).start()
        own_later_copy(ch).start()
        return carry

    lax.fori_loop(0, CHUNKS, start_own, 0)
    own_start = pl.multiple_of(c * rows, rows)
    copy_now = pltpu.make_async_copy(now_ref, acc.at[pl.ds(own_start, rows), :], own_now)
    copy_now.start()

    def relay(d, ch, side):
        origin = r + d * (1 - 2 * side)
        target = r - 1 + 2 * side

        @pl.when(in_line(origin))
        def _():
            line_copy(side, origin, ch, held.at[origin, ch], target).wait_recv()

            @pl.when(in_line(target))
            def _():
                line_copy(side, origin, ch, held.at[origin, ch], target).start()

    def first(ch, carry):
        now_copy(1, ch, own_piece(ch), across, across).wait_recv()
        now_copy(2, ch, slot(across, ch), across, partner).start()
        relay(1, ch, 0)
        relay(1, ch, 1)
        return carry

    lax.fori_loop(0, CHUNKS, first, 0)

    def settle(ch, carry):
        now_copy(0, ch, own_piece(ch), partner, partner).wait_recv()
        now_copy(2, ch, slot(across, ch), (partner + 2) % 4, partner).wait_recv()
        now_copy(2, ch, slot(across, ch), across, partner).wait_send()
        return carry

    lax.fori_loop(0, CHUNKS, settle, 0)
    copy_now.wait()

    def center(j, carry):
        at = pl.ds(pl.multiple_of(j * TILE, TILE), TILE)
        total = jnp.sum(acc[pl.ds(0, count), at], axis=0, keepdims=True)
        mean = total / jnp.float32(count)
        for block in range(4):
            part = (acc[pl.ds(block * rows, rows), at] - mean) / jnp.float32(count - 1)
            high, low = split(part.T)
            lhs[block, at, pl.ds(0, rows)] = high
            lhs[block, at, pl.ds(rows, rows)] = low
            lhs[block, at, pl.ds(2 * rows, rows)] = high
        return carry

    lax.fori_loop(0, feats // TILE, center, 0)

    def clear(j, carry):
        at = pl.ds(pl.multiple_of(j * TILE, TILE), TILE)
        acc[at, :] = jnp.zeros((TILE, cols), jnp.float32)
        return carry

    lax.fori_loop(0, feats // TILE, clear, 0)

    def multiply(origin, ch):
        high, low = split(held[origin, ch])
        rhs[pl.ds(0, rows), :] = high
        rhs[pl.ds(rows, rows), :] = high
        rhs[pl.ds(2 * rows, rows), :] = low

        def tile(i, carry):
            at = pl.ds(pl.multiple_of(i * TILE, TILE), TILE)
            acc[at, columns(ch)] += jnp.dot(
                lhs[origin, at, :], rhs[...], preferred_element_type=jnp.float32
            )
            return carry

        lax.fori_loop(0, feats // TILE, tile, 0)

    def step(t, carry):
        d, ch = t // CHUNKS, t % CHUNKS

        def one_side(side, inner):
            origin = r + d * (1 - 2 * side)

            @pl.when(in_line(origin) & (d + 1 - side > 0))
            def _():
                @pl.when(d == 0)
                def _():
                    own_later_copy(ch).wait()

                @pl.when(d >= 2)
                def _():
                    relay(d, ch, side)

                multiply(origin, ch)

            return inner

        lax.fori_loop(0, 2, one_side, 0)

        @pl.when(d == last)
        def _():
            out_copy(ch).start()

        return carry

    lax.fori_loop(0, n * CHUNKS, step, 0)

    def finish(ch, carry):
        now_copy(0, ch, own_piece(ch), c, partner).wait_send()
        now_copy(1, ch, own_piece(ch), c, across).wait_send()
        for side in range(2):
            target = r - 1 + 2 * side
            for d in range(n):
                origin = r + d * (1 - 2 * side)

                @pl.when(in_line(origin) & in_line(target))
                def _():
                    line_copy(side, origin, ch, held.at[origin, ch], target).wait_send()

        out_copy(ch).wait()
        return carry

    lax.fori_loop(0, CHUNKS, finish, 0)


def fused(n, grads_now, grads_later):
    rows, feats = grads_now.shape
    cols = grads_later.shape[1]
    return pl.pallas_call(
        functools.partial(kernel, n),
        out_shape=jax.ShapeDtypeStruct((feats, cols), jnp.float32),
        in_specs=[pl.BlockSpec(memory_space=pl.ANY)] * 2,
        out_specs=pl.BlockSpec(memory_space=pl.ANY),
        scratch_shapes=[
            pltpu.VMEM((feats, cols), jnp.float32),
            pltpu.VMEM((4, feats, 3 * rows), jnp.bfloat16),
            pltpu.VMEM((3 * rows, cols // CHUNKS), jnp.bfloat16),
            pltpu.VMEM((n, CHUNKS, rows, cols // CHUNKS), jnp.float32),
            pltpu.SemaphoreType.DMA,
            pltpu.SemaphoreType.DMA((CHUNKS,)),
            pltpu.SemaphoreType.DMA((3, CHUNKS)),
            pltpu.SemaphoreType.DMA((3, CHUNKS)),
            pltpu.SemaphoreType.DMA((2, n, CHUNKS)),
            pltpu.SemaphoreType.DMA((n, CHUNKS)),
            pltpu.SemaphoreType.DMA((CHUNKS,)),
        ],
        compiler_params=pltpu.CompilerParams(
            collective_id=0, has_side_effects=True, vmem_limit_bytes=58 * 2**20
        ),
        cost_estimate=pl.CostEstimate(
            flops=6 * n * rows * feats * cols,
            bytes_accessed=4 * (feats * cols + 2 * n * rows * cols),
            transcendentals=0,
        ),
    )(grads_now, grads_later)


def gathered(grads_now, grads_later):
    all_now = lax.all_gather(grads_now, "col", axis=0, tiled=True)
    count = all_now.shape[0]
    centered = all_now - jnp.mean(all_now, axis=0, keepdims=True)
    product = contract(centered, lax.all_gather(grads_later, "row", axis=0, tiled=True))
    return product / jnp.float32(count - 1)


def on_device(shape, grads_now, grads_later):
    n = shape["row"]
    rows, feats = grads_now.shape
    cols = grads_later.shape[1]
    fits = (
        shape["col"] == 4
        and n == 4
        and grads_later.shape[0] == rows
        and rows % (32 * CHUNKS) == 0
        and feats % TILE == 0
        and cols % (128 * CHUNKS) == 0
        and 4 * rows <= feats
        and feats == cols
    )
    if fits:
        return fused(n, grads_now, grads_later)
    return gathered(grads_now, grads_later)


def solution(mesh):
    placed = (P(("groups", "col"), "row"), P(("groups", "row"), "col"))
    return jax.shard_map(
        functools.partial(on_device, dict(mesh.shape)),
        mesh=mesh,
        in_specs=placed,
        out_specs=P(("groups", "row"), "col"),
        check_vma=False,
    )
```

```python
import functools

import jax
import jax.numpy as jnp
from jax import lax
from jax.experimental import pallas as pl
from jax.experimental.pallas import tpu as pltpu
from jax.sharding import PartitionSpec as P

MESH = pl.DeviceIdType.MESH
CHUNKS = 4
FIRST_MIB = 34
LAST_MIB = 10
TAIL = 1
TILE = 256


def contract(left, right):
    return lax.dot_general(
        left,
        right,
        (((0,), (0,)), ((), ())),
        precision=lax.Precision.HIGHEST,
        preferred_element_type=jnp.float32,
    )


def split(x):
    high = x.astype(jnp.bfloat16)
    low = (x - high.astype(jnp.float32)).astype(jnp.bfloat16)
    return high, low


def kernel(
    n, now_ref, later_ref, acc, lhs_last, rhs_last,
    lhs, rhs, held,
    own_now, own_later, now_send, now_recv, z_send, z_recv,
):
    r, c = lax.axis_index("row"), lax.axis_index("col")
    rows, feats = now_ref.shape
    cols = later_ref.shape[1]
    width = cols // CHUNKS
    piece = rows // CHUNKS
    count = 4 * rows
    partner = c + 1 - 2 * (c % 2)
    across = (c + 2) % 4

    def slot(block, ch):
        start = pl.multiple_of(block * rows + ch * piece, piece)
        return acc.at[pl.ds(start, piece), :]

    def columns(ch):
        return pl.ds(pl.multiple_of(ch * width, width), width)

    def now_copy(kind, ch, src, block, target):
        return pltpu.make_async_remote_copy(
            src_ref=src,
            dst_ref=slot(block, ch),
            send_sem=now_send.at[kind, ch],
            recv_sem=now_recv.at[kind, ch],
            device_id={"col": target},
            device_id_type=MESH,
        )

    def own_piece(ch):
        return now_ref.at[pl.ds(pl.multiple_of(ch * piece, piece), piece), :]

    def line_copy(side, origin, ch, src, target):
        return pltpu.make_async_remote_copy(
            src_ref=src,
            dst_ref=held.at[origin, ch],
            send_sem=z_send.at[side, origin, ch],
            recv_sem=z_recv.at[origin, ch],
            device_id={"row": target},
            device_id_type=MESH,
        )

    def in_line(i):
        return (i >= 0) & (i < n)

    def own_later_copy(ch):
        return pltpu.make_async_copy(later_ref.at[:, columns(ch)], held.at[r, ch], own_later.at[ch])

    barrier = pltpu.get_barrier_semaphore()
    pl.semaphore_signal(barrier, inc=1, device_id={"col": partner}, device_id_type=MESH)
    pl.semaphore_signal(barrier, inc=1, device_id={"col": across}, device_id_type=MESH)
    for side in range(2):
        target = r - 1 + 2 * side

        @pl.when(in_line(target))
        def _():
            pl.semaphore_signal(barrier, inc=1, device_id={"row": target}, device_id_type=MESH)

    pl.semaphore_wait(barrier, 2 + (r > 0).astype(jnp.int32) + (r < n - 1).astype(jnp.int32))

    def start_own(ch, carry):
        for side in range(2):
            target = r - 1 + 2 * side

            @pl.when(in_line(target))
            def _():
                line_copy(side, r, ch, later_ref.at[:, columns(ch)], target).start()

        now_copy(1, ch, own_piece(ch), c, across).start()
        now_copy(0, ch, own_piece(ch), c, partner).start()
        own_later_copy(ch).start()
        return carry

    lax.fori_loop(0, CHUNKS, start_own, 0)
    own_start = pl.multiple_of(c * rows, rows)
    copy_now = pltpu.make_async_copy(now_ref, acc.at[pl.ds(own_start, rows), :], own_now)
    copy_now.start()

    def relay(d, ch, side):
        origin = r + d * (1 - 2 * side)
        target = r - 1 + 2 * side

        @pl.when(in_line(origin))
        def _():
            line_copy(side, origin, ch, held.at[origin, ch], target).wait_recv()

            @pl.when(in_line(target))
            def _():
                line_copy(side, origin, ch, held.at[origin, ch], target).start()

    def first(ch, carry):
        now_copy(1, ch, own_piece(ch), across, across).wait_recv()
        now_copy(2, ch, slot(across, ch), across, partner).start()
        relay(1, ch, 0)
        relay(1, ch, 1)
        return carry

    lax.fori_loop(0, CHUNKS, first, 0)

    def settle(ch, carry):
        now_copy(0, ch, own_piece(ch), partner, partner).wait_recv()
        now_copy(2, ch, slot(across, ch), (partner + 2) % 4, partner).wait_recv()
        now_copy(2, ch, slot(across, ch), across, partner).wait_send()
        return carry

    lax.fori_loop(0, CHUNKS, settle, 0)
    copy_now.wait()

    def center(j, carry):
        at = pl.ds(pl.multiple_of(j * TILE, TILE), TILE)
        total = jnp.sum(acc[pl.ds(0, count), at], axis=0, keepdims=True)
        mean = total / jnp.float32(count)
        for block in range(4):
            part = (acc[pl.ds(block * rows, rows), at] - mean) / jnp.float32(count - 1)
            high, low = split(part.T)
            lhs[block, at, pl.ds(0, rows)] = high
            lhs[block, at, pl.ds(rows, rows)] = low
            lhs[block, at, pl.ds(2 * rows, rows)] = high

            @pl.when(block == n - 1 - r)
            def _():
                lhs_last[at, pl.ds(0, rows)] = high
                lhs_last[at, pl.ds(rows, rows)] = low
                lhs_last[at, pl.ds(2 * rows, rows)] = high

        return carry

    lax.fori_loop(0, feats // TILE, center, 0)

    def clear(j, carry):
        at = pl.ds(pl.multiple_of(j * TILE, TILE), TILE)
        acc[at, :] = jnp.zeros((TILE, cols), jnp.float32)
        return carry

    lax.fori_loop(0, feats // TILE, clear, 0)

    def place(to, origin, ch):
        high, low = split(held[origin, ch])
        to[pl.ds(0, rows), :] = high
        to[pl.ds(rows, rows), :] = high
        to[pl.ds(2 * rows, rows), :] = low

    def multiply(origin, ch):
        place(rhs, origin, ch)

        def tile(i, carry):
            at = pl.ds(pl.multiple_of(i * TILE, TILE), TILE)
            acc[at, columns(ch)] += jnp.dot(
                lhs[origin, at, :], rhs[...], preferred_element_type=jnp.float32
            )
            return carry

        lax.fori_loop(0, feats // TILE, tile, 0)

    def step(t, carry):
        d, ch = t // CHUNKS, t % CHUNKS

        def one_side(side, inner):
            origin = r + d * (1 - 2 * side)

            @pl.when(in_line(origin) & (d + 1 - side > 0))
            def _():
                @pl.when(d == 0)
                def _():
                    own_later_copy(ch).wait()

                @pl.when(d >= 2)
                def _():
                    relay(d, ch, side)

                @pl.when(t < n * CHUNKS - TAIL)
                def _():
                    multiply(origin, ch)

                @pl.when(t >= n * CHUNKS - TAIL)
                def _():
                    place(rhs_last.at[t - (n * CHUNKS - TAIL)], origin, ch)

            return inner

        lax.fori_loop(0, 2, one_side, 0)

        return carry

    lax.fori_loop(0, n * CHUNKS, step, 0)

    def finish(ch, carry):
        now_copy(0, ch, own_piece(ch), c, partner).wait_send()
        now_copy(1, ch, own_piece(ch), c, across).wait_send()
        for side in range(2):
            target = r - 1 + 2 * side
            for d in range(n):
                origin = r + d * (1 - 2 * side)

                @pl.when(in_line(origin) & in_line(target))
                def _():
                    line_copy(side, origin, ch, held.at[origin, ch], target).wait_send()

        return carry

    lax.fori_loop(0, CHUNKS, finish, 0)


def finish_out(n, acc, lhs, rhs, out_ref, block, sems, tile_sems):
    r = lax.axis_index("row")
    feats = acc.shape[0]
    width = acc.shape[1] // CHUNKS
    ready = CHUNKS - TAIL

    def columns(ch):
        return pl.ds(ch * width, width)

    for ch in range(ready):
        pltpu.make_async_copy(acc.at[:, columns(ch)], out_ref.at[:, columns(ch)], sems.at[ch]).start()

    for k in range(TAIL):
        ch = ready + k

        def tile_copy(i):
            at = pl.ds(pl.multiple_of(i * TILE, TILE), TILE)
            return pltpu.make_async_copy(
                block.at[k, at, :], out_ref.at[at, columns(ch)], tile_sems.at[k, i]
            )

        def tile(i, carry):
            at = pl.ds(pl.multiple_of(i * TILE, TILE), TILE)
            at_end = (r == 0) | (r == n - 1)

            @pl.when(at_end)
            def _():
                block[k, at, :] = acc[at, columns(ch)] + jnp.dot(
                    lhs[at, :], rhs[k], preferred_element_type=jnp.float32
                )

            @pl.when(jnp.logical_not(at_end))
            def _():
                block[k, at, :] = acc[at, columns(ch)]

            tile_copy(i).start()
            return carry

        lax.fori_loop(0, feats // TILE, tile, 0)

    for ch in range(ready):
        pltpu.make_async_copy(acc.at[:, columns(ch)], out_ref.at[:, columns(ch)], sems.at[ch]).wait()
    for k in range(TAIL):
        ch = ready + k

        def tile_wait(i, carry):
            at = pl.ds(pl.multiple_of(i * TILE, TILE), TILE)
            pltpu.make_async_copy(
                block.at[k, at, :], out_ref.at[at, columns(ch)], tile_sems.at[k, i]
            ).wait()
            return carry

        lax.fori_loop(0, feats // TILE, tile_wait, 0)


def fused(n, grads_now, grads_later):
    rows, feats = grads_now.shape
    cols = grads_later.shape[1]
    parts = pl.pallas_call(
        functools.partial(kernel, n),
        out_shape=(
            pltpu.VMEM((feats, cols), jnp.float32),
            pltpu.VMEM((feats, 3 * rows), jnp.bfloat16),
            pltpu.VMEM((TAIL, 3 * rows, cols // CHUNKS), jnp.bfloat16),
        ),
        in_specs=[pl.BlockSpec(memory_space=pl.ANY)] * 2,
        out_specs=(pl.BlockSpec(memory_space=pltpu.VMEM),) * 3,
        scratch_shapes=[
            pltpu.VMEM((4, feats, 3 * rows), jnp.bfloat16),
            pltpu.VMEM((3 * rows, cols // CHUNKS), jnp.bfloat16),
            pltpu.VMEM((n, CHUNKS, rows, cols // CHUNKS), jnp.float32),
            pltpu.SemaphoreType.DMA,
            pltpu.SemaphoreType.DMA((CHUNKS,)),
            pltpu.SemaphoreType.DMA((3, CHUNKS)),
            pltpu.SemaphoreType.DMA((3, CHUNKS)),
            pltpu.SemaphoreType.DMA((2, n, CHUNKS)),
            pltpu.SemaphoreType.DMA((n, CHUNKS)),
        ],
        compiler_params=pltpu.CompilerParams(
            collective_id=0, has_side_effects=True, vmem_limit_bytes=FIRST_MIB * 2**20
        ),
        cost_estimate=pl.CostEstimate(
            flops=6 * n * rows * feats * cols,
            bytes_accessed=4 * (feats * cols + 2 * n * rows * cols),
            transcendentals=0,
        ),
    )(grads_now, grads_later)
    parts = [pltpu.with_memory_space_constraint(part, pltpu.VMEM) for part in parts]
    return pl.pallas_call(
        functools.partial(finish_out, n),
        out_shape=jax.ShapeDtypeStruct((feats, cols), jnp.float32),
        in_specs=[pl.BlockSpec(memory_space=pltpu.VMEM)] * 3,
        out_specs=pl.BlockSpec(memory_space=pl.ANY),
        scratch_shapes=[
            pltpu.VMEM((TAIL, feats, cols // CHUNKS), jnp.float32),
            pltpu.SemaphoreType.DMA((CHUNKS,)),
            pltpu.SemaphoreType.DMA((TAIL, feats // TILE)),
        ],
        compiler_params=pltpu.CompilerParams(vmem_limit_bytes=LAST_MIB * 2**20),
    )(*parts)


def gathered(grads_now, grads_later):
    all_now = lax.all_gather(grads_now, "col", axis=0, tiled=True)
    count = all_now.shape[0]
    centered = all_now - jnp.mean(all_now, axis=0, keepdims=True)
    product = contract(centered, lax.all_gather(grads_later, "row", axis=0, tiled=True))
    return product / jnp.float32(count - 1)


def on_device(shape, grads_now, grads_later):
    n = shape["row"]
    rows, feats = grads_now.shape
    cols = grads_later.shape[1]
    fits = (
        shape["col"] == 4
        and n == 4
        and grads_later.shape[0] == rows
        and rows % (8 * CHUNKS) == 0
        and feats % TILE == 0
        and cols % (128 * CHUNKS) == 0
        and 4 * rows <= feats
        and feats == cols
    )
    if fits:
        return fused(n, grads_now, grads_later)
    return gathered(grads_now, grads_later)


def solution(mesh):
    placed = (P(("groups", "col"), "row"), P(("groups", "row"), "col"))
    return jax.shard_map(
        functools.partial(on_device, dict(mesh.shape)),
        mesh=mesh,
        in_specs=placed,
        out_specs=P(("groups", "row"), "col"),
        check_vma=False,
    )
```

```python
import functools

import jax
import jax.numpy as jnp
from jax import lax
from jax.experimental import pallas as pl
from jax.experimental.pallas import tpu as pltpu
from jax.sharding import PartitionSpec as P

MESH = pl.DeviceIdType.MESH
CHUNKS = 4
HALF = CHUNKS // 2
FIRST_MIB = 34
LAST_MIB = 10
TAIL = 1
TILE = 256


def contract(left, right):
    return lax.dot_general(
        left,
        right,
        (((0,), (0,)), ((), ())),
        precision=lax.Precision.HIGHEST,
        preferred_element_type=jnp.float32,
    )


def split(x):
    high = x.astype(jnp.bfloat16)
    low = (x - high.astype(jnp.float32)).astype(jnp.bfloat16)
    return high, low


def kernel(
    n, now_ref, later_ref, acc, lhs_last, rhs_last,
    lhs, rhs, held,
    own_now, own_later, now_send, now_recv, z_send, z_recv,
):
    r, c = lax.axis_index("row"), lax.axis_index("col")
    rows, feats = now_ref.shape
    cols = later_ref.shape[1]
    width = cols // CHUNKS
    piece = rows // CHUNKS
    count = 4 * rows
    partner = c + 1 - 2 * (c % 2)
    across = (c + 2) % 4

    def slot(block, ch):
        start = pl.multiple_of(block * rows + ch * piece, piece)
        return acc.at[pl.ds(start, piece), :]

    def columns(ch):
        return pl.ds(pl.multiple_of(ch * width, width), width)

    def now_copy(kind, ch, src, block, target):
        return pltpu.make_async_remote_copy(
            src_ref=src,
            dst_ref=slot(block, ch),
            send_sem=now_send.at[kind, ch],
            recv_sem=now_recv.at[kind, ch],
            device_id={"col": target},
            device_id_type=MESH,
        )

    def own_piece(ch):
        return now_ref.at[pl.ds(pl.multiple_of(ch * piece, piece), piece), :]

    def line_copy(side, origin, ch, src, target):
        return pltpu.make_async_remote_copy(
            src_ref=src,
            dst_ref=held.at[origin, ch],
            send_sem=z_send.at[side, origin, ch],
            recv_sem=z_recv.at[origin, ch],
            device_id={"row": target},
            device_id_type=MESH,
        )

    def in_line(i):
        return (i >= 0) & (i < n)

    def own_later_copy(ch):
        return pltpu.make_async_copy(later_ref.at[:, columns(ch)], held.at[r, ch], own_later.at[ch])

    barrier = pltpu.get_barrier_semaphore()
    pl.semaphore_signal(barrier, inc=1, device_id={"col": partner}, device_id_type=MESH)
    pl.semaphore_signal(barrier, inc=1, device_id={"col": across}, device_id_type=MESH)
    for side in range(2):
        target = r - 1 + 2 * side

        @pl.when(in_line(target))
        def _():
            pl.semaphore_signal(barrier, inc=1, device_id={"row": target}, device_id_type=MESH)

    pl.semaphore_wait(barrier, 2 + (r > 0).astype(jnp.int32) + (r < n - 1).astype(jnp.int32))

    def own_line(side, ch):
        return line_copy(side, r, ch, later_ref.at[:, columns(ch)], r - 1 + 2 * side)

    def start_own(ch, carry):
        for side in range(2):

            @pl.when(in_line(r - 1 + 2 * side) & (ch < HALF))
            def _():
                own_line(side, ch).start()

        now_copy(1, ch, own_piece(ch), c, across).start()
        now_copy(0, ch, own_piece(ch), c, partner).start()
        own_later_copy(ch).start()
        return carry

    lax.fori_loop(0, CHUNKS, start_own, 0)
    own_start = pl.multiple_of(c * rows, rows)
    copy_now = pltpu.make_async_copy(now_ref, acc.at[pl.ds(own_start, rows), :], own_now)
    copy_now.start()

    def relay(d, ch, side):
        origin = r + d * (1 - 2 * side)
        target = r - 1 + 2 * side

        @pl.when(in_line(origin))
        def _():
            line_copy(side, origin, ch, held.at[origin, ch], target).wait_recv()

            @pl.when(in_line(target))
            def _():
                line_copy(side, origin, ch, held.at[origin, ch], target).start()

    def first(ch, carry):
        for side in range(2):

            @pl.when(in_line(r - 1 + 2 * side) & (ch < HALF))
            def _():
                own_line(side, ch).wait_send()
                own_line(side, ch + HALF).start()

        relay(1, ch, 0)
        relay(1, ch, 1)
        return carry

    lax.fori_loop(0, CHUNKS, first, 0)

    def cross(ch, carry):
        now_copy(1, ch, own_piece(ch), across, across).wait_recv()
        now_copy(2, ch, slot(across, ch), across, partner).start()
        return carry

    lax.fori_loop(0, CHUNKS, cross, 0)

    def settle(ch, carry):
        now_copy(0, ch, own_piece(ch), partner, partner).wait_recv()
        now_copy(2, ch, slot(across, ch), (partner + 2) % 4, partner).wait_recv()
        now_copy(2, ch, slot(across, ch), across, partner).wait_send()
        return carry

    lax.fori_loop(0, CHUNKS, settle, 0)
    copy_now.wait()

    def center(j, carry):
        at = pl.ds(pl.multiple_of(j * TILE, TILE), TILE)
        total = jnp.sum(acc[pl.ds(0, count), at], axis=0, keepdims=True)
        mean = total / jnp.float32(count)
        for block in range(4):
            part = (acc[pl.ds(block * rows, rows), at] - mean) / jnp.float32(count - 1)
            high, low = split(part.T)
            lhs[block, at, pl.ds(0, rows)] = high
            lhs[block, at, pl.ds(rows, rows)] = low
            lhs[block, at, pl.ds(2 * rows, rows)] = high

            @pl.when(block == n - 1 - r)
            def _():
                lhs_last[at, pl.ds(0, rows)] = high
                lhs_last[at, pl.ds(rows, rows)] = low
                lhs_last[at, pl.ds(2 * rows, rows)] = high

        return carry

    lax.fori_loop(0, feats // TILE, center, 0)

    def clear(j, carry):
        at = pl.ds(pl.multiple_of(j * TILE, TILE), TILE)
        acc[at, :] = jnp.zeros((TILE, cols), jnp.float32)
        return carry

    lax.fori_loop(0, feats // TILE, clear, 0)

    def place(to, origin, ch):
        high, low = split(held[origin, ch])
        to[pl.ds(0, rows), :] = high
        to[pl.ds(rows, rows), :] = high
        to[pl.ds(2 * rows, rows), :] = low

    def multiply(origin, ch):
        place(rhs, origin, ch)

        def tile(i, carry):
            at = pl.ds(pl.multiple_of(i * TILE, TILE), TILE)
            acc[at, columns(ch)] += jnp.dot(
                lhs[origin, at, :], rhs[...], preferred_element_type=jnp.float32
            )
            return carry

        lax.fori_loop(0, feats // TILE, tile, 0)

    def step(t, carry):
        d, ch = t // CHUNKS, t % CHUNKS

        def one_side(side, inner):
            origin = r + d * (1 - 2 * side)

            @pl.when(in_line(origin) & (d + 1 - side > 0))
            def _():
                @pl.when(d == 0)
                def _():
                    own_later_copy(ch).wait()

                @pl.when(d >= 2)
                def _():
                    relay(d, ch, side)

                @pl.when(t < n * CHUNKS - TAIL)
                def _():
                    multiply(origin, ch)

                @pl.when(t >= n * CHUNKS - TAIL)
                def _():
                    place(rhs_last.at[t - (n * CHUNKS - TAIL)], origin, ch)

            return inner

        lax.fori_loop(0, 2, one_side, 0)

        return carry

    lax.fori_loop(0, n * CHUNKS, step, 0)

    def finish(ch, carry):
        now_copy(0, ch, own_piece(ch), c, partner).wait_send()
        now_copy(1, ch, own_piece(ch), c, across).wait_send()
        for side in range(2):
            target = r - 1 + 2 * side
            for d in range(n):
                origin = r + d * (1 - 2 * side)

                @pl.when(in_line(origin) & in_line(target) & (d * CHUNKS + ch >= HALF))
                def _():
                    line_copy(side, origin, ch, held.at[origin, ch], target).wait_send()

        return carry

    lax.fori_loop(0, CHUNKS, finish, 0)


def finish_out(n, acc, lhs, rhs, out_ref, block, sems, tile_sems):
    r = lax.axis_index("row")
    feats = acc.shape[0]
    width = acc.shape[1] // CHUNKS
    ready = CHUNKS - TAIL

    def columns(ch):
        return pl.ds(ch * width, width)

    for ch in range(ready):
        pltpu.make_async_copy(acc.at[:, columns(ch)], out_ref.at[:, columns(ch)], sems.at[ch]).start()

    for k in range(TAIL):
        ch = ready + k

        def tile_copy(i):
            at = pl.ds(pl.multiple_of(i * TILE, TILE), TILE)
            return pltpu.make_async_copy(
                block.at[k, at, :], out_ref.at[at, columns(ch)], tile_sems.at[k, i]
            )

        def tile(i, carry):
            at = pl.ds(pl.multiple_of(i * TILE, TILE), TILE)
            at_end = (r == 0) | (r == n - 1)

            @pl.when(at_end)
            def _():
                block[k, at, :] = acc[at, columns(ch)] + jnp.dot(
                    lhs[at, :], rhs[k], preferred_element_type=jnp.float32
                )

            @pl.when(jnp.logical_not(at_end))
            def _():
                block[k, at, :] = acc[at, columns(ch)]

            tile_copy(i).start()
            return carry

        lax.fori_loop(0, feats // TILE, tile, 0)

    for ch in range(ready):
        pltpu.make_async_copy(acc.at[:, columns(ch)], out_ref.at[:, columns(ch)], sems.at[ch]).wait()
    for k in range(TAIL):
        ch = ready + k

        def tile_wait(i, carry):
            at = pl.ds(pl.multiple_of(i * TILE, TILE), TILE)
            pltpu.make_async_copy(
                block.at[k, at, :], out_ref.at[at, columns(ch)], tile_sems.at[k, i]
            ).wait()
            return carry

        lax.fori_loop(0, feats // TILE, tile_wait, 0)


def fused(n, grads_now, grads_later):
    rows, feats = grads_now.shape
    cols = grads_later.shape[1]
    parts = pl.pallas_call(
        functools.partial(kernel, n),
        out_shape=(
            pltpu.VMEM((feats, cols), jnp.float32),
            pltpu.VMEM((feats, 3 * rows), jnp.bfloat16),
            pltpu.VMEM((TAIL, 3 * rows, cols // CHUNKS), jnp.bfloat16),
        ),
        in_specs=[pl.BlockSpec(memory_space=pl.ANY)] * 2,
        out_specs=(pl.BlockSpec(memory_space=pltpu.VMEM),) * 3,
        scratch_shapes=[
            pltpu.VMEM((4, feats, 3 * rows), jnp.bfloat16),
            pltpu.VMEM((3 * rows, cols // CHUNKS), jnp.bfloat16),
            pltpu.VMEM((n, CHUNKS, rows, cols // CHUNKS), jnp.float32),
            pltpu.SemaphoreType.DMA,
            pltpu.SemaphoreType.DMA((CHUNKS,)),
            pltpu.SemaphoreType.DMA((3, CHUNKS)),
            pltpu.SemaphoreType.DMA((3, CHUNKS)),
            pltpu.SemaphoreType.DMA((2, n, CHUNKS)),
            pltpu.SemaphoreType.DMA((n, CHUNKS)),
        ],
        compiler_params=pltpu.CompilerParams(
            collective_id=0, has_side_effects=True, vmem_limit_bytes=FIRST_MIB * 2**20
        ),
        cost_estimate=pl.CostEstimate(
            flops=6 * n * rows * feats * cols,
            bytes_accessed=4 * (feats * cols + 2 * n * rows * cols),
            transcendentals=0,
        ),
    )(grads_now, grads_later)
    parts = [pltpu.with_memory_space_constraint(part, pltpu.VMEM) for part in parts]
    return pl.pallas_call(
        functools.partial(finish_out, n),
        out_shape=jax.ShapeDtypeStruct((feats, cols), jnp.float32),
        in_specs=[pl.BlockSpec(memory_space=pltpu.VMEM)] * 3,
        out_specs=pl.BlockSpec(memory_space=pl.ANY),
        scratch_shapes=[
            pltpu.VMEM((TAIL, feats, cols // CHUNKS), jnp.float32),
            pltpu.SemaphoreType.DMA((CHUNKS,)),
            pltpu.SemaphoreType.DMA((TAIL, feats // TILE)),
        ],
        compiler_params=pltpu.CompilerParams(vmem_limit_bytes=LAST_MIB * 2**20),
    )(*parts)


def gathered(grads_now, grads_later):
    all_now = lax.all_gather(grads_now, "col", axis=0, tiled=True)
    count = all_now.shape[0]
    centered = all_now - jnp.mean(all_now, axis=0, keepdims=True)
    product = contract(centered, lax.all_gather(grads_later, "row", axis=0, tiled=True))
    return product / jnp.float32(count - 1)


def on_device(shape, grads_now, grads_later):
    n = shape["row"]
    rows, feats = grads_now.shape
    cols = grads_later.shape[1]
    fits = (
        shape["col"] == 4
        and n == 4
        and grads_later.shape[0] == rows
        and rows % (8 * CHUNKS) == 0
        and feats % TILE == 0
        and cols % (128 * CHUNKS) == 0
        and 4 * rows <= feats
        and feats == cols
    )
    if fits:
        return fused(n, grads_now, grads_later)
    return gathered(grads_now, grads_later)


def solution(mesh):
    placed = (P(("groups", "col"), "row"), P(("groups", "row"), "col"))
    return jax.shard_map(
        functools.partial(on_device, dict(mesh.shape)),
        mesh=mesh,
        in_specs=placed,
        out_specs=P(("groups", "row"), "col"),
        check_vma=False,
    )
```
